32 devices in a mesh: shot: 2 (over x), gx: 16 (over z, y, core).
Axes of the slice: x: 2, y: 2, z: 4, core: 2. Of those that a mesh axis runs over, the one named last changes fastest.
Arguments:
- source_field: float32 [512, 16, 128], P(('shot', 'gx')), parts along dimension 0, may hold values from -6 to 6
- source_prior: float32 [512, 16, 128], P(('shot', 'gx')), parts along dimension 0, may hold values from -6 to 6
- receiver_field: float32 [512, 16, 128], P(('shot', 'gx')), parts along dimension 0, may hold values from -6 to 6
- receiver_prior: float32 [512, 16, 128], P(('shot', 'gx')), parts along dimension 0, may hold values from -6 to 6
- stiffness: float32 [256, 16, 128], P('gx'), may hold values from 0.02 to 0.085
- buoyancy: float32 [256, 16, 128], P('gx'), may hold values from 0.5 to 2
- wavelet: float32 [32, 8], P('shot'), parts along dimension 0, may hold values from -6 to 6
- fire_step: int32 [32], P('shot'), parts along dimension 0, may hold values from 0 to 7
- shot_cell: int32 [32], P('shot'), parts along dimension 0, may hold values from 0 to 4095
- receiver_cell: int32 [4096], P('shot'), parts along dimension 0, may hold values from 0 to 4095
- traces: float32 [16, 2048], P('shot', 'gx'), parts along dimension 0, may hold values from -6 to 6
Outputs:
- image_sum: float32 [66, 256, 16, 128], P('shot', 'gx'), parts along dimension 0
The draws below stay inside these ranges and needn't reach their ends.
There are 2 independent parts, one for each index of `shot`. The reference program is written for one: setup_inputs(seed, part) draws one part's arguments, and reference() takes and returns one part's arrays. A program takes and returns all parts, laid end to end along the dimension named above; an argument that names none is the same for every part. Nothing has to cross between parts.
All inputs are finite; a program needn't handle non-finite values.
Results may differ from the reference program's by a relative error of at most 0.0003.
Values sent between devices are 32-bit elements; how exact they have to be, the bound alone decides.
A program may use at most 64 MiB of HBM per device.

```python
import math
import jax
import jax.numpy as jnp

NY = 16
NZ = 128
STEPS = 8
IMG_EVERY = 4
NOFF = 33
SURFACE = 4
NSRC = 16
HALF = 16
NX = 256
NREC = 2048


def set_ends(array, key, smallest, top_value):
    longest = array.shape.index(max(array.shape))
    spots = []
    for shift in (0, 1):
        where = [jax.random.randint(jax.random.fold_in(key, axis), (), 0, length) for axis, length in enumerate(array.shape)]
        where[longest] = (where[longest] + shift) % array.shape[longest]
        spots.append(tuple(where))
    return array.at[spots[0]].set(smallest).at[spots[1]].set(top_value)


def block_levels(stream_key, shape, split, smallest, largest):
    def one(axis_at, blocks):
        steps = jax.random.uniform(jax.random.fold_in(jax.random.fold_in(stream_key, 6), axis_at), (blocks,), jnp.float32, smallest / len(split), largest / len(split))
        return jnp.repeat(jnp.exp(steps), shape[axis_at] // blocks).reshape((-1,) + (1,) * (len(shape) - axis_at - 1))

    gain = one(*split[0])
    for cut in split[1:]:
        gain = gain * one(*cut)
    return gain


def gaussian(stream_key, dims, deviation, limit, cuts=(), kind=jnp.bfloat16):
    loudness = block_levels(stream_key, dims, cuts, -0.22, 0.18) if cuts else 1.0
    entries = jax.random.normal(stream_key, dims, jnp.float32) * deviation * loudness
    return jnp.minimum(jnp.maximum(entries, -limit), limit).astype(kind)


def setup_inputs(seed: int = 0, part: int = 0) -> dict:
    key_list = jax.random.split(jax.random.key(seed), 12)
    part_keys = jax.random.split(jax.random.fold_in(key_list[11], part), 12)
    return {
        "source_field": gaussian(part_keys[0], (NX, NY, NZ), 1.0, 6.0, ((0, 16),), jnp.float32),
        "source_prior": gaussian(part_keys[1], (NX, NY, NZ), 1.0, 6.0, ((0, 16),), jnp.float32),
        "receiver_field": gaussian(part_keys[2], (NX, NY, NZ), 1.0, 6.0, ((0, 16),), jnp.float32),
        "receiver_prior": gaussian(part_keys[3], (NX, NY, NZ), 1.0, 6.0, ((0, 16),), jnp.float32),
        "stiffness": jnp.clip(jnp.exp(math.log(0.085) - 1.446919 * jax.random.uniform(key_list[4], (NX, NY, NZ), jnp.float32) ** block_levels(key_list[4], (NX, NY, NZ), ((0, 16),), -0.2, 0.2)), 0.02, 0.085),
        "buoyancy": jnp.clip(jnp.exp(math.log(2.0) - 1.3862944 * jax.random.uniform(key_list[5], (NX, NY, NZ), jnp.float32) ** block_levels(key_list[5], (NX, NY, NZ), ((0, 16),), -0.2, 0.2)), 0.5, 2.0),
        "wavelet": gaussian(part_keys[6], (NSRC, STEPS), 1.0, 6.0, (), jnp.float32),
        "fire_step": set_ends(jax.random.randint(part_keys[7], (NSRC,), 0, STEPS), jax.random.fold_in(part_keys[7], 1), 0, STEPS - 1).astype(jnp.int32),
        "shot_cell": set_ends(jax.random.randint(part_keys[8], (NSRC,), 0, NX * NY), jax.random.fold_in(part_keys[8], 1), 0, (NX * NY) - 1).astype(jnp.int32),
        "receiver_cell": set_ends(jax.random.randint(part_keys[9], (NREC,), 0, NX * NY), jax.random.fold_in(part_keys[9], 1), 0, (NX * NY) - 1).astype(jnp.int32),
        "traces": gaussian(part_keys[10], (STEPS, NREC), 1.0, 6.0, ((1, 16),), jnp.float32),
    }


stencil_weights = (1.6, -0.2, 8.0 / 315.0, -1.0 / 560.0)


def window(padded, direction, offset, extent):
    starts = [4, 4, 4]
    starts[direction] = starts[direction] + offset
    return padded[starts[0]:starts[0] + extent[0], starts[1]:starts[1] + extent[1], starts[2]:starts[2] + extent[2]]


def laplace(wavefield, buoyant):
    extent = (wavefield.shape[0] - 8, wavefield.shape[1], wavefield.shape[2])
    padded_field = jnp.pad(wavefield, ((0, 0), (4, 4), (4, 4)))
    padded_buoyant = jnp.pad(buoyant, ((0, 0), (4, 4), (4, 4)))
    centre_field = window(padded_field, 0, 0, extent)
    centre_buoyant = window(padded_buoyant, 0, 0, extent)
    accumulated = jnp.zeros(extent, jnp.float32)
    for direction in range(3):
        for distance in range(4):
            for orientation in (1, -1):
                other_field = window(padded_field, direction, orientation * (distance + 1), extent)
                other_buoyant = window(padded_buoyant, direction, orientation * (distance + 1), extent)
                accumulated = accumulated + stencil_weights[distance] * (0.5 * (centre_buoyant + other_buoyant)) * (other_field - centre_field)
    return accumulated


def inject_plane(cell_index, amounts, start_row, span_rows, lateral):
    inline = cell_index // lateral
    crossline = cell_index % lateral
    relative = inline - start_row
    inside = (relative >= 0) & (relative < span_rows)
    target = jnp.where(inside, relative * lateral + crossline, span_rows * lateral)
    summed = jax.ops.segment_sum(jnp.where(inside, amounts, 0.0), target, num_segments=span_rows * lateral + 1)
    return summed[:span_rows * lateral].reshape(span_rows, lateral)


def wavelet_amounts(wavelet, fire_step, moment):
    delays = moment - fire_step
    choose = jnp.arange(wavelet.shape[1], dtype=jnp.int32)[None, :] == delays[:, None]
    return jnp.sum(jnp.where(choose, wavelet, 0.0), axis=1)


def advance(current, prior_field, buoyant, stiff_cells, source_term):
    centre_cells = current[4:current.shape[0] - 4]
    updated = 2.0 * centre_cells - prior_field + stiff_cells * laplace(current, buoyant)
    return updated.at[:, :, SURFACE].add(source_term)


def correlate(lag_source, lag_receiver, span_rows):
    pieces = []
    for offset_index in range(NOFF):
        lag_shift = offset_index - HALF
        pieces.append(lag_source[HALF - lag_shift:HALF - lag_shift + span_rows] * lag_receiver[HALF + lag_shift:HALF + lag_shift + span_rows])
    return jnp.stack(pieces, 0)


def reference(source_field, source_prior, receiver_field, receiver_prior, stiffness, buoyancy, wavelet, fire_step, shot_cell, receiver_cell, traces):
    pad_stencil = ((4, 4), (0, 0), (0, 0))
    pad_lag = ((HALF, HALF), (0, 0), (0, 0))
    padded_buoyant = jnp.pad(buoyancy, pad_stencil)
    source_now, source_before = source_field, source_prior
    receiver_now, receiver_before = receiver_field, receiver_prior
    image_sum = None
    for moment in range(STEPS + 1):
        if moment % IMG_EVERY == 0:
            product = correlate(jnp.pad(source_now, pad_lag), jnp.pad(receiver_now, pad_lag), NX)
            image_sum = product if moment == 0 else image_sum + product
        if moment < STEPS:
            source_term = inject_plane(shot_cell, wavelet_amounts(wavelet, fire_step, moment), 0, NX, NY)
            receiver_term = inject_plane(receiver_cell, traces[STEPS - 1 - moment], 0, NX, NY)
            source_next = advance(jnp.pad(source_now, pad_stencil), source_before, padded_buoyant, stiffness, source_term)
            receiver_next = advance(jnp.pad(receiver_now, pad_stencil), receiver_before, padded_buoyant, stiffness, receiver_term)
            source_before, source_now = source_now, source_next
            receiver_before, receiver_now = receiver_now, receiver_next
    return image_sum
```

```python
import functools

import jax
import jax.numpy as jnp
from jax import lax
from jax.experimental import pallas as pl
from jax.experimental.pallas import tpu as pltpu
from jax.sharding import PartitionSpec as P

STEPS = 8
IMG_EVERY = 4
NOFF = 33
SURFACE = 4
HALF = 16
REACH = 4
AXIS = "gx"

stencil_weights = (1.6, -0.2, 8.0 / 315.0, -1.0 / 560.0)


def split3(x):
    hi = x.astype(jnp.bfloat16)
    rest = x - hi.astype(jnp.float32)
    mid = rest.astype(jnp.bfloat16)
    low = (rest - mid.astype(jnp.float32)).astype(jnp.bfloat16)
    return hi, mid, low


def propagate(
    count,
    s_ref, sp_ref, r_ref, rp_ref, k_ref, b_ref, wave_ref, fire_ref, shot_ref, rcell_ref, trace_ref,
    out_ref,
    lev, bx, coef, plane_s, plane_r, gathered, wpad, ipad,
    send_sem, recv_sem, bsend_sem, brecv_sem, tsend_sem, trecv_sem,
):
    me = lax.axis_index(AXIS)
    rows, lateral, depth = s_ref.shape
    H, E = HALF, REACH
    has_left, has_right = me > 0, me < count - 1
    rounds = out_ref.shape[0] - 1

    def level(n):
        return out_ref.at[n // IMG_EVERY] if n % IMG_EVERY == 0 else lev.at[n]

    barrier = pltpu.get_barrier_semaphore()

    def greet(j, c):
        @pl.when(j != me)
        def _():
            pl.semaphore_signal(barrier, inc=1, device_id={AXIS: j}, device_id_type=pl.DeviceIdType.MESH)
        return c

    lax.fori_loop(0, count, greet, 0)

    first = level(0)

    def fill(i, c):
        first[H + i, 0] = s_ref[i]
        first[H + i, 1] = r_ref[i]
        bx[E + i] = b_ref[i]
        return c

    lax.fori_loop(0, rows, fill, 0)
    zero_row = jnp.zeros((2, lateral, depth), jnp.float32)

    def blank(lo_halo):
        for n in range(STEPS + 1):
            wide = H if n % IMG_EVERY == 0 else E
            at = H - wide if lo_halo else H + rows
            target = level(n)

            def one(i, c, target=target, at=at):
                target[at + i] = zero_row
                return c

            lax.fori_loop(0, wide, one, 0)
        for i in range(E):
            bx[i if lo_halo else E + rows + i] = jnp.zeros((lateral, depth), jnp.float32)

    @pl.when(jnp.logical_not(has_left))
    def _():
        blank(True)

    @pl.when(jnp.logical_not(has_right))
    def _():
        blank(False)

    gathered[me] = trace_ref[...]
    pl.semaphore_wait(barrier, count - 1)

    def halo_copy(n, side, chunk):
        if n == STEPS and chunk == 1:
            skip, size = E, H - E
        else:
            skip, size = chunk * E, E
        if side == 0:
            src, dst, to = H + rows - skip - size, H - skip - size, me + 1
        else:
            src, dst, to = H + skip, H + rows + skip, me - 1
        ref = level(n)
        return pltpu.make_async_remote_copy(
            src_ref=ref.at[pl.ds(src, size)], dst_ref=ref.at[pl.ds(dst, size)],
            send_sem=send_sem.at[n, side, chunk], recv_sem=recv_sem.at[n, side, chunk],
            device_id={AXIS: to}, device_id_type=pl.DeviceIdType.MESH)

    def b_copy(side):
        src, dst, to = (rows, 0, me + 1) if side == 0 else (E, E + rows, me - 1)
        return pltpu.make_async_remote_copy(
            src_ref=bx.at[pl.ds(src, E)], dst_ref=bx.at[pl.ds(dst, E)],
            send_sem=bsend_sem.at[side], recv_sem=brecv_sem.at[side],
            device_id={AXIS: to}, device_id_type=pl.DeviceIdType.MESH)

    def start(make):
        @pl.when(has_right)
        def _():
            make(0).start()

        @pl.when(has_left)
        def _():
            make(1).start()

    def wait_recv(make):
        @pl.when(has_left)
        def _():
            make(0).wait_recv()

        @pl.when(has_right)
        def _():
            make(1).wait_recv()

    def wait_send(make):
        @pl.when(has_right)
        def _():
            make(0).wait_send()

        @pl.when(has_left)
        def _():
            make(1).wait_send()

    def t_send(j):
        return pltpu.make_async_remote_copy(
            src_ref=trace_ref, dst_ref=gathered.at[me],
            send_sem=tsend_sem.at[j], recv_sem=trecv_sem.at[me],
            device_id={AXIS: j}, device_id_type=pl.DeviceIdType.MESH)

    def t_recv(j):
        return pltpu.make_async_remote_copy(
            src_ref=trace_ref, dst_ref=gathered.at[j],
            send_sem=tsend_sem.at[j], recv_sem=trecv_sem.at[j],
            device_id={AXIS: j}, device_id_type=pl.DeviceIdType.MESH)

    def others(act):
        def body(j, c):
            @pl.when(j != me)
            def _():
                act(j)
            return c

        lax.fori_loop(0, count, body, 0)

    others(lambda j: t_send(j).start())
    start(b_copy)
    start(lambda side: halo_copy(0, side, 0))

    lane = lax.broadcasted_iota(jnp.int32, (lateral, depth), 1)
    cross = lax.broadcasted_iota(jnp.int32, (lateral, depth), 0)

    def flat_coefs(i, c):
        b = bx[E + i]
        stiff = k_ref[i]
        total = jnp.zeros_like(b)
        for base, axis, index, length in ((8, 0, cross, lateral), (16, 1, lane, depth)):
            for k in range(1, REACH + 1):
                for s in (1, -1):
                    inside = index < length - k if s == 1 else index >= k
                    other = jnp.where(inside, pltpu.roll(b, (-s * k) % length, axis), 0.0)
                    t = (0.5 * stencil_weights[k - 1]) * (b + other)
                    total = total + t
                    coef[base + 2 * (k - 1) + (s < 0), i] = jnp.where(inside, stiff * t, 0.0)
        coef[24, i] = total
        return c

    lax.fori_loop(0, rows, flat_coefs, 0)

    def inline_coefs(i, c):
        b = bx[E + i]
        stiff = k_ref[i]
        total = coef[24, i]
        for k in range(1, REACH + 1):
            for s in (1, -1):
                t = (0.5 * stencil_weights[k - 1]) * (b + bx[E + i + s * k])
                total = total + t
                coef[2 * (k - 1) + (s < 0), i] = stiff * t
        coef[24, i] = 2.0 - stiff * total
        return c

    lax.fori_loop(E, rows - E, inline_coefs, 0)

    cells = rows * lateral
    cell_id = lax.broadcasted_iota(jnp.int32, (cells, 128), 0) + me * cells
    quiet = jnp.zeros((128 - 3 * STEPS, 128), jnp.bfloat16)

    def spread(cell_row, amounts):
        hot = jnp.where(cell_id == cell_row, 1.0, 0.0).astype(jnp.bfloat16)
        parts = jnp.concatenate(list(split3(amounts)) + [quiet], axis=0)
        return lax.dot_general(hot, parts, (((1,), (1,)), ((), ())), preferred_element_type=jnp.float32)

    def fold(p):
        return p + pltpu.roll(p, 128 - STEPS, 1) + pltpu.roll(p, 128 - 2 * STEPS, 1)

    shots, samples = wave_ref.shape
    wpad[...] = jnp.zeros_like(wpad)
    wpad[0:shots, 0:samples] = wave_ref[...]
    ipad[...] = jnp.full(ipad.shape, -1, jnp.int32)
    ipad[0:1, 0:shots] = fire_ref[...]
    ipad[1:2, 0:shots] = shot_ref[...]
    wave_t = wpad[...].T
    delay = lax.broadcasted_iota(jnp.int32, (STEPS, 128), 0) - ipad[0:1, :]
    amounts = jnp.zeros((STEPS, 128), jnp.float32)
    for d in range(samples):
        amounts = amounts + jnp.where(delay == d, wave_t[d : d + 1, :], 0.0)
    plane_s[...] = fold(spread(ipad[1:2, :], amounts))

    others(lambda j: t_recv(j).wait_recv())
    plane_r[...] = jnp.zeros_like(plane_r)

    def absorb(j, c):
        plane_r[...] += spread(rcell_ref[pl.ds(j, 1), :], gathered[j])
        return c

    lax.fori_loop(0, count, absorb, 0)
    plane_r[...] = fold(plane_r[...])

    wait_recv(b_copy)
    lax.fori_loop(0, E, inline_coefs, 0)
    lax.fori_loop(rows - E, rows, inline_coefs, 0)

    def advance(n, lo, hi):
        now, nxt = level(n), level(n + 1)

        def one(i, c):
            at = H + i
            for f in range(2):
                v = now[at, f]
                if n == 0:
                    before = (sp_ref, rp_ref)[f][i]
                else:
                    before = level(n - 1)[at, f]
                acc = [coef[24, i] * v - before]
                for base, axis, length in ((8, 0, lateral), (16, 1, depth)):
                    part = None
                    for k in range(1, REACH + 1):
                        for s in (1, -1):
                            term = coef[base + 2 * (k - 1) + (s < 0), i] * pltpu.roll(v, (-s * k) % length, axis)
                            part = term if part is None else part + term
                    acc.append(part)
                part = None
                for k in range(1, REACH + 1):
                    for s in (1, -1):
                        term = coef[2 * (k - 1) + (s < 0), i] * now[at + s * k, f]
                        part = term if part is None else part + term
                acc.append(part)
                plane, column = (plane_s, n) if f == 0 else (plane_r, STEPS - 1 - n)
                p = plane[pl.ds(pl.multiple_of(i * lateral, lateral), lateral), :]
                p = jnp.where(lane == SURFACE, pltpu.roll(p, (SURFACE - column) % 128, 1), 0.0)
                nxt[at, f] = (acc[0] + acc[1]) + (acc[2] + acc[3]) + p
            return c

        lax.fori_loop(lo, hi, one, 0)

    sent = [(0, 0)]
    for n in range(STEPS):
        wait_recv(lambda side: halo_copy(n, side, 0))
        advance(n, 0, E)
        advance(n, rows - E, rows)
        start(lambda side: halo_copy(n + 1, side, 0))
        sent.append((n + 1, 0))
        chunk = n % IMG_EVERY
        if chunk > 0:
            imaged = n - chunk
            start(lambda side: halo_copy(imaged, side, chunk))
            sent.append((imaged, chunk))
        advance(n, E, rows - E)
    start(lambda side: halo_copy(STEPS, side, 1))
    sent.append((STEPS, 1))
    for n, chunk in sent:
        if n == STEPS or chunk > 0:
            wait_recv(lambda side: halo_copy(n, side, chunk))
    wait_send(b_copy)
    for n, chunk in sent:
        wait_send(lambda side: halo_copy(n, side, chunk))
    others(lambda j: t_send(j).wait_send())


def imaging(per, rows, levels_ref, image_ref):
    block = pl.program_id(0)
    for jj in range(per):
        shift = block * per + jj - HALF

        def one(i, c, jj=jj, shift=shift):
            total = None
            for n in range(levels_ref.shape[0]):
                product = levels_ref[n, HALF + i - shift, 0] * levels_ref[n, HALF + i + shift, 1]
                total = product if total is None else total + product
            image_ref[jj, i] = total
            return c

        lax.fori_loop(0, rows, one, 0, unroll=True)


def solution(mesh):
    count = mesh.shape[AXIS]

    def local(sf, sp, rf, rp, stiff, buoy, wavelet, fire, shot, rcell, traces):
        rows, lateral, depth = sf.shape
        rounds = STEPS // IMG_EVERY
        wide = rows + 2 * HALF
        vm = pl.BlockSpec(memory_space=pltpu.VMEM)
        levels = pl.pallas_call(
            functools.partial(propagate, count),
            out_shape=jax.ShapeDtypeStruct((rounds + 1, wide, 2, lateral, depth), jnp.float32),
            in_specs=[vm] * 11,
            out_specs=vm,
            scratch_shapes=[
                pltpu.VMEM((STEPS, wide, 2, lateral, depth), jnp.float32),
                pltpu.VMEM((rows + 2 * REACH, lateral, depth), jnp.float32),
                pltpu.VMEM((25, rows, lateral, depth), jnp.float32),
                pltpu.VMEM((rows * lateral, 128), jnp.float32),
                pltpu.VMEM((rows * lateral, 128), jnp.float32),
                pltpu.VMEM((count,) + traces.shape, jnp.float32),
                pltpu.VMEM((128, 128), jnp.float32),
                pltpu.VMEM((8, 128), jnp.int32),
                pltpu.SemaphoreType.DMA((STEPS + 1, 2, 4)),
                pltpu.SemaphoreType.DMA((STEPS + 1, 2, 4)),
                pltpu.SemaphoreType.DMA((2,)),
                pltpu.SemaphoreType.DMA((2,)),
                pltpu.SemaphoreType.DMA((count,)),
                pltpu.SemaphoreType.DMA((count,)),
            ],
            compiler_params=pltpu.CompilerParams(
                collective_id=0, has_side_effects=True, vmem_limit_bytes=40 * 1024 * 1024),
        )(sf, sp, rf, rp, stiff, buoy, wavelet, fire.reshape(1, -1), shot.reshape(1, -1),
          rcell.reshape(count, traces.shape[1]), traces)
        per = 3
        return pl.pallas_call(
            functools.partial(imaging, per, rows),
            grid=(NOFF // per,),
            out_shape=jax.ShapeDtypeStruct((NOFF, rows, lateral, depth), jnp.float32),
            in_specs=[vm],
            out_specs=pl.BlockSpec((per, rows, lateral, depth), lambda j: (j, 0, 0, 0)),
            compiler_params=pltpu.CompilerParams(vmem_limit_bytes=24 * 1024 * 1024),
        )(levels)

    placed = (
        P(("shot", AXIS), None, None),
        P(("shot", AXIS), None, None),
        P(("shot", AXIS), None, None),
        P(("shot", AXIS), None, None),
        P(AXIS, None, None),
        P(AXIS, None, None),
        P("shot", None),
        P("shot"),
        P("shot"),
        P("shot"),
        P("shot", AXIS),
    )
    return jax.shard_map(
        local, mesh=mesh, in_specs=placed, out_specs=P("shot", AXIS, None, None), check_vma=False
    )
```

```python
import functools

import jax
import jax.numpy as jnp
from jax import lax
from jax.experimental import pallas as pl
from jax.experimental.pallas import tpu as pltpu
from jax.sharding import PartitionSpec as P

STEPS = 8
IMG_EVERY = 4
NOFF = 33
SURFACE = 4
HALF = 16
REACH = 4
AXIS = "gx"
UNROLL = 4
GROUP = 3

stencil_weights = (1.6, -0.2, 8.0 / 315.0, -1.0 / 560.0)


def split3(x):
    hi = x.astype(jnp.bfloat16)
    rest = x - hi.astype(jnp.float32)
    mid = rest.astype(jnp.bfloat16)
    low = (rest - mid.astype(jnp.float32)).astype(jnp.bfloat16)
    return hi, mid, low


def propagate(
    count,
    s_hbm, sp_hbm, r_hbm, rp_hbm, k_hbm, b_hbm, wave_hbm, fire_hbm, shot_hbm, rcell_hbm, trace_hbm,
    out_ref,
    lev, bx, coef, plane_s, plane_r, gathered, wpad, ipad,
    prior, k_ref, wave_ref, fire_ref, shot_ref, rcell_ref, trace_ref,
    in_sem, out_sem, send_sem, recv_sem, bsend_sem, brecv_sem, tsend_sem, trecv_sem,
):
    me = lax.axis_index(AXIS)
    rows, lateral, depth = s_hbm.shape
    H, E = HALF, REACH
    has_left, has_right = me > 0, me < count - 1

    def level(n):
        return lev.at[n]

    def save(n):
        return pltpu.make_async_copy(lev.at[n], out_ref.at[n // IMG_EVERY], out_sem.at[n // IMG_EVERY])

    first = level(0)
    loads = [
        pltpu.make_async_copy(src, dst, in_sem.at[i])
        for i, (src, dst) in enumerate((
            (trace_hbm, trace_ref),
            (b_hbm, bx.at[pl.ds(E, rows)]),
            (s_hbm, first.at[pl.ds(H, rows), 0]),
            (r_hbm, first.at[pl.ds(H, rows), 1]),
            (k_hbm, k_ref),
            (wave_hbm, wave_ref),
            (fire_hbm, fire_ref),
            (shot_hbm, shot_ref),
            (rcell_hbm, rcell_ref),
            (sp_hbm, prior.at[0]),
            (rp_hbm, prior.at[1]),
        ))
    ]
    for copy in loads:
        copy.start()

    barrier = pltpu.get_barrier_semaphore()

    def greet(j, c):
        @pl.when(j != me)
        def _():
            pl.semaphore_signal(barrier, inc=1, device_id={AXIS: j}, device_id_type=pl.DeviceIdType.MESH)
        return c

    lax.fori_loop(0, count, greet, 0)

    zero_row = jnp.zeros((2, lateral, depth), jnp.float32)

    def blank(lo_halo):
        for n in range(STEPS + 1):
            wide = H if n % IMG_EVERY == 0 else E
            at = H - wide if lo_halo else H + rows
            target = level(n)

            def one(i, c, target=target, at=at):
                target[at + i] = zero_row
                return c

            lax.fori_loop(0, wide, one, 0)
        for i in range(E):
            bx[i if lo_halo else E + rows + i] = jnp.zeros((lateral, depth), jnp.float32)

    @pl.when(jnp.logical_not(has_left))
    def _():
        blank(True)

    @pl.when(jnp.logical_not(has_right))
    def _():
        blank(False)

    pl.semaphore_wait(barrier, count - 1)
    for copy in loads:
        copy.wait()
    gathered[me] = trace_ref[...]

    def halo_copy(n, side, chunk):
        if n == STEPS and chunk == 1:
            skip, size = E, H - E
        else:
            skip, size = chunk * E, E
        if side == 0:
            src, dst, to = H + rows - skip - size, H - skip - size, me + 1
        else:
            src, dst, to = H + skip, H + rows + skip, me - 1
        ref = level(n)
        return pltpu.make_async_remote_copy(
            src_ref=ref.at[pl.ds(src, size)], dst_ref=ref.at[pl.ds(dst, size)],
            send_sem=send_sem.at[n, side, chunk], recv_sem=recv_sem.at[n, side, chunk],
            device_id={AXIS: to}, device_id_type=pl.DeviceIdType.MESH)

    def b_copy(side):
        src, dst, to = (rows, 0, me + 1) if side == 0 else (E, E + rows, me - 1)
        return pltpu.make_async_remote_copy(
            src_ref=bx.at[pl.ds(src, E)], dst_ref=bx.at[pl.ds(dst, E)],
            send_sem=bsend_sem.at[side], recv_sem=brecv_sem.at[side],
            device_id={AXIS: to}, device_id_type=pl.DeviceIdType.MESH)

    def start(make):
        @pl.when(has_right)
        def _():
            make(0).start()

        @pl.when(has_left)
        def _():
            make(1).start()

    def wait_recv(make):
        @pl.when(has_left)
        def _():
            make(0).wait_recv()

        @pl.when(has_right)
        def _():
            make(1).wait_recv()

    def wait_send(make):
        @pl.when(has_right)
        def _():
            make(0).wait_send()

        @pl.when(has_left)
        def _():
            make(1).wait_send()

    def t_send(j):
        return pltpu.make_async_remote_copy(
            src_ref=trace_ref, dst_ref=gathered.at[me],
            send_sem=tsend_sem.at[j], recv_sem=trecv_sem.at[me],
            device_id={AXIS: j}, device_id_type=pl.DeviceIdType.MESH)

    def t_recv(j):
        return pltpu.make_async_remote_copy(
            src_ref=trace_ref, dst_ref=gathered.at[j],
            send_sem=tsend_sem.at[j], recv_sem=trecv_sem.at[j],
            device_id={AXIS: j}, device_id_type=pl.DeviceIdType.MESH)

    def others(act):
        def body(j, c):
            @pl.when(j != me)
            def _():
                act(j)
            return c

        lax.fori_loop(0, count, body, 0)

    others(lambda j: t_send(j).start())
    start(b_copy)
    start(lambda side: halo_copy(0, side, 0))

    lane = lax.broadcasted_iota(jnp.int32, (lateral, depth), 1)
    cross = lax.broadcasted_iota(jnp.int32, (lateral, depth), 0)

    def flat_coefs(i, c):
        b = bx[E + i]
        stiff = k_ref[i]
        total = jnp.zeros_like(b)
        for base, axis, index, length in ((8, 0, cross, lateral), (16, 1, lane, depth)):
            for k in range(1, REACH + 1):
                for s in (1, -1):
                    inside = index < length - k if s == 1 else index >= k
                    other = jnp.where(inside, pltpu.roll(b, (-s * k) % length, axis), 0.0)
                    t = (0.5 * stencil_weights[k - 1]) * (b + other)
                    total = total + t
                    coef[base + 2 * (k - 1) + (s < 0), i] = jnp.where(inside, stiff * t, 0.0)
        coef[24, i] = total
        return c

    lax.fori_loop(0, rows, flat_coefs, 0)

    def inline_coefs(i, c):
        b = bx[E + i]
        stiff = k_ref[i]
        total = coef[24, i]
        for k in range(1, REACH + 1):
            for s in (1, -1):
                t = (0.5 * stencil_weights[k - 1]) * (b + bx[E + i + s * k])
                total = total + t
                coef[2 * (k - 1) + (s < 0), i] = stiff * t
        coef[24, i] = 2.0 - stiff * total
        return c

    lax.fori_loop(E, rows - E, inline_coefs, 0)

    cells = rows * lateral
    cell_id = lax.broadcasted_iota(jnp.int32, (cells, 128), 0) + me * cells
    quiet = jnp.zeros((128 - 3 * STEPS, 128), jnp.bfloat16)

    def spread(cell_row, amounts):
        hot = jnp.where(cell_id == cell_row, 1.0, 0.0).astype(jnp.bfloat16)
        parts = jnp.concatenate(list(split3(amounts)) + [quiet], axis=0)
        return lax.dot_general(hot, parts, (((1,), (1,)), ((), ())), preferred_element_type=jnp.float32)

    def fold(p):
        return p + pltpu.roll(p, 128 - STEPS, 1) + pltpu.roll(p, 128 - 2 * STEPS, 1)

    samples, shots = wave_ref.shape
    wpad[...] = jnp.zeros_like(wpad)
    wpad[0:samples, 0:shots] = wave_ref[...]
    ipad[...] = jnp.full(ipad.shape, -1, jnp.int32)
    ipad[0:1, 0:shots] = fire_ref[...]
    ipad[1:2, 0:shots] = shot_ref[...]
    delay = lax.broadcasted_iota(jnp.int32, (STEPS, 128), 0) - ipad[0:1, :]
    amounts = jnp.zeros((STEPS, 128), jnp.float32)
    for d in range(samples):
        amounts = amounts + jnp.where(delay == d, wpad[d : d + 1, :], 0.0)
    plane_s[...] = fold(spread(ipad[1:2, :], amounts))

    others(lambda j: t_recv(j).wait_recv())
    plane_r[...] = jnp.zeros_like(plane_r)

    def absorb(j, c):
        plane_r[...] += spread(rcell_ref[pl.ds(j, 1), :], gathered[j])
        return c

    lax.fori_loop(0, count, absorb, 0)
    plane_r[...] = fold(plane_r[...])

    wait_recv(b_copy)
    lax.fori_loop(0, E, inline_coefs, 0)
    lax.fori_loop(rows - E, rows, inline_coefs, 0)

    def advance(n, size, row):
        now, nxt = level(n), level(n + 1)

        def one(q, c):
            i = row(q)
            at = H + i
            for f in range(2):
                v = now[at, f]
                if n == 0:
                    before = prior[f, i]
                else:
                    before = level(n - 1)[at, f]
                acc = [coef[24, i] * v - before]
                for base, axis, length in ((8, 0, lateral), (16, 1, depth)):
                    part = None
                    for k in range(1, REACH + 1):
                        for s in (1, -1):
                            term = coef[base + 2 * (k - 1) + (s < 0), i] * pltpu.roll(v, (-s * k) % length, axis)
                            part = term if part is None else part + term
                    acc.append(part)
                part = None
                for k in range(1, REACH + 1):
                    for s in (1, -1):
                        term = coef[2 * (k - 1) + (s < 0), i] * now[at + s * k, f]
                        part = term if part is None else part + term
                acc.append(part)
                plane, column = (plane_s, n) if f == 0 else (plane_r, STEPS - 1 - n)
                p = plane[pl.ds(pl.multiple_of(i * lateral, lateral), lateral), :]
                p = jnp.where(lane == SURFACE, pltpu.roll(p, (SURFACE - column) % 128, 1), 0.0)
                nxt[at, f] = (acc[0] + acc[1]) + (acc[2] + acc[3]) + p
            return c

        lax.fori_loop(0, size, one, 0, unroll=UNROLL)

    sent = [(0, 0)]
    for n in range(STEPS):
        wait_recv(lambda side: halo_copy(n, side, 0))
        advance(n, 2 * E, lambda q: jnp.where(q < E, q, rows - 2 * E + q))
        start(lambda side: halo_copy(n + 1, side, 0))
        sent.append((n + 1, 0))
        chunk = n % IMG_EVERY
        if chunk > 0:
            imaged = n - chunk
            start(lambda side: halo_copy(imaged, side, chunk))
            sent.append((imaged, chunk))
        advance(n, rows - 2 * E, lambda q: q + E)
        if n >= IMG_EVERY and chunk == 0:
            for c in range(1, HALF // E):
                wait_recv(lambda side: halo_copy(n - IMG_EVERY, side, c))
            save(n - IMG_EVERY).start()
    start(lambda side: halo_copy(STEPS, side, 1))
    sent.append((STEPS, 1))
    for c in range(1, HALF // E):
        wait_recv(lambda side: halo_copy(STEPS - IMG_EVERY, side, c))
    save(STEPS - IMG_EVERY).start()
    for c in range(2):
        wait_recv(lambda side: halo_copy(STEPS, side, c))
    save(STEPS).start()
    wait_send(b_copy)
    for n, chunk in sent:
        wait_send(lambda side: halo_copy(n, side, chunk))
    others(lambda j: t_send(j).wait_send())
    for n in range(0, STEPS + 1, IMG_EVERY):
        save(n).wait()


def imaging(levels_hbm, image_hbm, levels, image, in_sem, out_sem):
    rounds, rows = levels.shape[0], image.shape[1]
    loads = [pltpu.make_async_copy(levels_hbm.at[n], levels.at[n], in_sem.at[n]) for n in range(rounds)]
    for copy in loads:
        copy.start()
    for copy in loads:
        copy.wait()
    stores = []
    for start in range(0, NOFF, GROUP):
        for j in range(start, start + GROUP):
            shift = j - HALF

            def one(i, c, j=j, shift=shift):
                total = None
                for n in range(rounds):
                    product = levels[n, HALF + i - shift, 0] * levels[n, HALF + i + shift, 1]
                    total = product if total is None else total + product
                image[j, i] = total
                return c

            lax.fori_loop(0, rows, one, 0, unroll=True)
        part = pl.ds(start, GROUP)
        stores.append(pltpu.make_async_copy(image.at[part], image_hbm.at[part], out_sem.at[start // GROUP]))
        stores[-1].start()
    for copy in stores:
        copy.wait()


def solution(mesh):
    count = mesh.shape[AXIS]

    def local(sf, sp, rf, rp, stiff, buoy, wavelet, fire, shot, rcell, traces):
        rows, lateral, depth = sf.shape
        rounds = STEPS // IMG_EVERY
        wide = rows + 2 * HALF
        levels = pl.pallas_call(
            functools.partial(propagate, count),
            out_shape=jax.ShapeDtypeStruct((rounds + 1, wide, 2, lateral, depth), jnp.float32),
            in_specs=[pl.BlockSpec(memory_space=pltpu.HBM)] * 11,
            out_specs=pl.BlockSpec(memory_space=pltpu.HBM),
            scratch_shapes=[
                pltpu.VMEM((STEPS + 1, wide, 2, lateral, depth), jnp.float32),
                pltpu.VMEM((rows + 2 * REACH, lateral, depth), jnp.float32),
                pltpu.VMEM((25, rows, lateral, depth), jnp.float32),
                pltpu.VMEM((rows * lateral, 128), jnp.float32),
                pltpu.VMEM((rows * lateral, 128), jnp.float32),
                pltpu.VMEM((count,) + traces.shape, jnp.float32),
                pltpu.VMEM((wavelet.shape[1], 128), jnp.float32),
                pltpu.VMEM((8, 128), jnp.int32),
                pltpu.VMEM((2, rows, lateral, depth), jnp.float32),
                pltpu.VMEM((rows, lateral, depth), jnp.float32),
                pltpu.VMEM(wavelet.shape[::-1], jnp.float32),
                pltpu.VMEM((1,) + fire.shape, jnp.int32),
                pltpu.VMEM((1,) + shot.shape, jnp.int32),
                pltpu.VMEM((count, traces.shape[1]), jnp.int32),
                pltpu.VMEM(traces.shape, jnp.float32),
                pltpu.SemaphoreType.DMA((11,)),
                pltpu.SemaphoreType.DMA((rounds + 1,)),
                pltpu.SemaphoreType.DMA((STEPS + 1, 2, 4)),
                pltpu.SemaphoreType.DMA((STEPS + 1, 2, 4)),
                pltpu.SemaphoreType.DMA((2,)),
                pltpu.SemaphoreType.DMA((2,)),
                pltpu.SemaphoreType.DMA((count,)),
                pltpu.SemaphoreType.DMA((count,)),
            ],
            compiler_params=pltpu.CompilerParams(
                collective_id=0, has_side_effects=True, vmem_limit_bytes=62 * 1024 * 1024),
        )(sf, sp, rf, rp, stiff, buoy, wavelet.T, fire.reshape(1, -1), shot.reshape(1, -1),
          rcell.reshape(count, traces.shape[1]), traces)
        hbm = pl.BlockSpec(memory_space=pltpu.HBM)
        return pl.pallas_call(
            imaging,
            out_shape=jax.ShapeDtypeStruct((NOFF, rows, lateral, depth), jnp.float32),
            in_specs=[hbm],
            out_specs=hbm,
            scratch_shapes=[
                pltpu.VMEM(levels.shape, jnp.float32),
                pltpu.VMEM((NOFF, rows, lateral, depth), jnp.float32),
                pltpu.SemaphoreType.DMA((rounds + 1,)),
                pltpu.SemaphoreType.DMA((NOFF // GROUP,)),
            ],
            compiler_params=pltpu.CompilerParams(vmem_limit_bytes=62 * 1024 * 1024),
        )(levels)

    placed = (
        P(("shot", AXIS), None, None),
        P(("shot", AXIS), None, None),
        P(("shot", AXIS), None, None),
        P(("shot", AXIS), None, None),
        P(AXIS, None, None),
        P(AXIS, None, None),
        P("shot", None),
        P("shot"),
        P("shot"),
        P("shot"),
        P("shot", AXIS),
    )
    return jax.shard_map(
        local, mesh=mesh, in_specs=placed, out_specs=P("shot", AXIS, None, None), check_vma=False
    )
```

```python
import functools

import jax
import jax.numpy as jnp
from jax import lax
from jax.experimental import pallas as pl
from jax.experimental.pallas import tpu as pltpu
from jax.sharding import PartitionSpec as P

STEPS = 8
IMG_EVERY = 4
NOFF = 33
SURFACE = 4
HALF = 16
REACH = 4
AXIS = "gx"
UNROLL = 4
GROUP = 3

stencil_weights = (1.6, -0.2, 8.0 / 315.0, -1.0 / 560.0)


def split3(x):
    hi = x.astype(jnp.bfloat16)
    rest = x - hi.astype(jnp.float32)
    mid = rest.astype(jnp.bfloat16)
    low = (rest - mid.astype(jnp.float32)).astype(jnp.bfloat16)
    return hi, mid, low


def propagate(
    count,
    s_hbm, sp_hbm, r_hbm, rp_hbm, k_hbm, b_hbm, wave_hbm, fire_hbm, shot_hbm, rcell_hbm, trace_hbm,
    out_ref,
    lev, bx, coef, plane_s, plane_r, gathered, wpad, ipad,
    prior, k_ref, wave_ref, fire_ref, shot_ref, rcell_ref, trace_ref,
    in_sem, out_sem, send_sem, recv_sem, bsend_sem, brecv_sem, tsend_sem, trecv_sem,
):
    me = lax.axis_index(AXIS)
    rows, lateral, depth = s_hbm.shape
    H, E, D = HALF, REACH, 2 * REACH
    has_left, has_right = me > 0, me < count - 1

    def level(n):
        return lev.at[n]

    def save(n):
        return pltpu.make_async_copy(lev.at[n], out_ref.at[n // IMG_EVERY], out_sem.at[n // IMG_EVERY])

    first = level(0)
    loads = [
        pltpu.make_async_copy(src, dst, in_sem.at[i])
        for i, (src, dst) in enumerate((
            (trace_hbm, trace_ref),
            (b_hbm, bx.at[pl.ds(D, rows)]),
            (s_hbm, first.at[pl.ds(H, rows), 0]),
            (r_hbm, first.at[pl.ds(H, rows), 1]),
            (k_hbm, k_ref.at[pl.ds(E, rows)]),
            (wave_hbm, wave_ref),
            (fire_hbm, fire_ref),
            (shot_hbm, shot_ref),
            (rcell_hbm, rcell_ref),
            (sp_hbm, prior.at[pl.ds(E, rows), 0]),
            (rp_hbm, prior.at[pl.ds(E, rows), 1]),
        ))
    ]
    for copy in loads:
        copy.start()

    barrier = pltpu.get_barrier_semaphore()

    def greet(j, c):
        @pl.when(j != me)
        def _():
            pl.semaphore_signal(barrier, inc=1, device_id={AXIS: j}, device_id_type=pl.DeviceIdType.MESH)
        return c

    lax.fori_loop(0, count, greet, 0)

    zero_row = jnp.zeros((2, lateral, depth), jnp.float32)

    def blank(lo_halo):
        for n in range(0, STEPS + 1, 2):
            wide = H if n % IMG_EVERY == 0 else D
            at = H - wide if lo_halo else H + rows
            target = level(n)

            def one(i, c, target=target, at=at):
                target[at + i] = zero_row
                return c

            lax.fori_loop(0, wide, one, 0)

        def sides(i, c):
            at = i if lo_halo else E + rows + i
            prior[at] = zero_row
            k_ref[at] = zero_row[0]
            for part in range(2):
                bx[(part * E + i) if lo_halo else (D + rows + part * E + i)] = zero_row[0]
            return c

        lax.fori_loop(0, E, sides, 0)

    @pl.when(jnp.logical_not(has_left))
    def _():
        blank(True)

    @pl.when(jnp.logical_not(has_right))
    def _():
        blank(False)

    pl.semaphore_wait(barrier, count - 1)
    for copy in loads:
        copy.wait()
    gathered[me] = trace_ref[...]

    def shifted(ref, own, skip, size, side, send, recv):
        if side == 0:
            src, dst, to = own + rows - skip - size, own - skip - size, me + 1
        else:
            src, dst, to = own + skip, own + rows + skip, me - 1
        return pltpu.make_async_remote_copy(
            src_ref=ref.at[pl.ds(src, size)], dst_ref=ref.at[pl.ds(dst, size)],
            send_sem=send, recv_sem=recv,
            device_id={AXIS: to}, device_id_type=pl.DeviceIdType.MESH)

    def halo_copy(n, side, chunk):
        skip, size = (0, D) if chunk == 0 else (D, H - D)
        return shifted(level(n), H, skip, size, side, send_sem.at[n, side, chunk], recv_sem.at[n, side, chunk])

    def model_copy(which, side):
        ref, own, size = ((bx, D, D), (k_ref, E, E), (prior, E, E))[which]
        return shifted(ref, own, 0, size, side, bsend_sem.at[which, side], brecv_sem.at[which, side])

    def start(make, sides=(0, 1)):
        for side in sides:
            @pl.when((has_right, has_left)[side])
            def _(side=side):
                make(side).start()

    def wait_recv(make):
        @pl.when(has_left)
        def _():
            make(0).wait_recv()

        @pl.when(has_right)
        def _():
            make(1).wait_recv()

    def wait_send(make):
        @pl.when(has_right)
        def _():
            make(0).wait_send()

        @pl.when(has_left)
        def _():
            make(1).wait_send()

    def t_send(j):
        return pltpu.make_async_remote_copy(
            src_ref=trace_ref, dst_ref=gathered.at[me],
            send_sem=tsend_sem.at[j], recv_sem=trecv_sem.at[me],
            device_id={AXIS: j}, device_id_type=pl.DeviceIdType.MESH)

    def t_recv(j):
        return pltpu.make_async_remote_copy(
            src_ref=trace_ref, dst_ref=gathered.at[j],
            send_sem=tsend_sem.at[j], recv_sem=trecv_sem.at[j],
            device_id={AXIS: j}, device_id_type=pl.DeviceIdType.MESH)

    def others(act):
        def body(j, c):
            @pl.when(j != me)
            def _():
                act(j)
            return c

        lax.fori_loop(0, count, body, 0)

    others(lambda j: t_send(j).start())
    for which in range(2):
        start(lambda side: model_copy(which, side))
    start(lambda side: halo_copy(0, side, 0))
    start(lambda side: model_copy(2, side))

    lane = lax.broadcasted_iota(jnp.int32, (lateral, depth), 1)
    cross = lax.broadcasted_iota(jnp.int32, (lateral, depth), 0)

    def flat_coefs(i, c):
        b = bx[E + i]
        stiff = k_ref[i]
        total = jnp.zeros_like(b)
        for base, axis, index, length in ((8, 0, cross, lateral), (16, 1, lane, depth)):
            for k in range(1, REACH + 1):
                for s in (1, -1):
                    inside = index < length - k if s == 1 else index >= k
                    other = jnp.where(inside, pltpu.roll(b, (-s * k) % length, axis), 0.0)
                    t = (0.5 * stencil_weights[k - 1]) * (b + other)
                    total = total + t
                    coef[base + 2 * (k - 1) + (s < 0), i] = jnp.where(inside, stiff * t, 0.0)
        coef[24, i] = total
        return c

    lax.fori_loop(E, E + rows, flat_coefs, 0, unroll=2)

    def inline_coefs(i, c):
        b = bx[E + i]
        stiff = k_ref[i]
        total = coef[24, i]
        for k in range(1, REACH + 1):
            for s in (1, -1):
                t = (0.5 * stencil_weights[k - 1]) * (b + bx[E + i + s * k])
                total = total + t
                coef[2 * (k - 1) + (s < 0), i] = stiff * t
        coef[24, i] = 2.0 - stiff * total
        return c

    lax.fori_loop(D, rows, inline_coefs, 0, unroll=2)

    cells = (rows + D) * lateral
    cell_id = lax.broadcasted_iota(jnp.int32, (cells, 128), 0) + (me * rows - E) * lateral
    quiet = jnp.zeros((128 - 3 * STEPS, 128), jnp.bfloat16)

    def spread(cell_row, amounts):
        hot = jnp.where(cell_id == cell_row, 1.0, 0.0).astype(jnp.bfloat16)
        parts = jnp.concatenate(list(split3(amounts)) + [quiet], axis=0)
        return lax.dot_general(hot, parts, (((1,), (1,)), ((), ())), preferred_element_type=jnp.float32)

    def fold(p):
        return p + pltpu.roll(p, 128 - STEPS, 1) + pltpu.roll(p, 128 - 2 * STEPS, 1)

    samples, shots = wave_ref.shape
    wpad[...] = jnp.zeros_like(wpad)
    wpad[0:samples, 0:shots] = wave_ref[...]
    ipad[...] = jnp.full(ipad.shape, -1, jnp.int32)
    ipad[0:1, 0:shots] = fire_ref[...]
    ipad[1:2, 0:shots] = shot_ref[...]
    delay = lax.broadcasted_iota(jnp.int32, (STEPS, 128), 0) - ipad[0:1, :]
    amounts = jnp.zeros((STEPS, 128), jnp.float32)
    for d in range(samples):
        amounts = amounts + jnp.where(delay == d, wpad[d : d + 1, :], 0.0)
    plane_s[...] = fold(spread(ipad[1:2, :], amounts))

    others(lambda j: t_recv(j).wait_recv())
    plane_r[...] = jnp.zeros_like(plane_r)

    def absorb(j, c):
        plane_r[...] += spread(rcell_ref[pl.ds(j, 1), :], gathered[j])
        return c

    lax.fori_loop(0, count, absorb, 0)
    plane_r[...] = fold(plane_r[...])

    wait_recv(lambda side: model_copy(0, side))
    wait_recv(lambda side: model_copy(1, side))

    def outer(q):
        return jnp.where(q < E, q, rows + q)

    def outer_coefs(q, c):
        flat_coefs(outer(q), c)
        inline_coefs(outer(q), c)
        return c

    def edge_coefs(q, c):
        return inline_coefs(jnp.where(q < E, q + E, rows - E + q), c)

    lax.fori_loop(0, D, outer_coefs, 0, unroll=2)
    lax.fori_loop(0, D, edge_coefs, 0, unroll=2)

    def advance(n, size, row):
        now, nxt = level(n), level(n + 1)

        def one(q, c):
            i = row(q)
            at = H - E + i
            for f in range(2):
                v = now[at, f]
                if n == 0:
                    before = prior[i, f]
                else:
                    before = level(n - 1)[at, f]
                acc = [coef[24, i] * v - before]
                for base, axis, length in ((8, 0, lateral), (16, 1, depth)):
                    part = None
                    for k in range(1, REACH + 1):
                        for s in (1, -1):
                            term = coef[base + 2 * (k - 1) + (s < 0), i] * pltpu.roll(v, (-s * k) % length, axis)
                            part = term if part is None else part + term
                    acc.append(part)
                part = None
                for k in range(1, REACH + 1):
                    for s in (1, -1):
                        term = coef[2 * (k - 1) + (s < 0), i] * now[at + s * k, f]
                        part = term if part is None else part + term
                acc.append(part)
                plane, column = (plane_s, n) if f == 0 else (plane_r, STEPS - 1 - n)
                p = plane[pl.ds(pl.multiple_of(i * lateral, lateral), lateral), :]
                p = jnp.where(lane == SURFACE, pltpu.roll(p, (SURFACE - column) % 128, 1), 0.0)
                nxt[at, f] = (acc[0] + acc[1]) + (acc[2] + acc[3]) + p
            return c

        lax.fori_loop(0, size, one, 0, unroll=UNROLL)

    sent = [(0, 0)]
    half = rows // 2
    for n in range(0, STEPS, 2):
        advance(n, rows - D, lambda q: D + q)
        wait_recv(lambda side: halo_copy(n, side, 0))
        if n == 0:
            wait_recv(lambda side: model_copy(2, side))
        advance(n, 2 * D, lambda q: jnp.where(q < D, q, rows - D + q))
        advance(n + 1, half, lambda q: E + q)
        start(lambda side: halo_copy(n + 2, side, 0), (1,))
        if n + 2 == STEPS:
            start(lambda side: halo_copy(n + 2, side, 1), (0,))
        advance(n + 1, rows - half, lambda q: E + half + q)
        start(lambda side: halo_copy(n + 2, side, 0), (0,))
        sent.append((n + 2, 0))
        if n + 2 == STEPS:
            start(lambda side: halo_copy(n + 2, side, 1), (1,))
            sent.append((n + 2, 1))
        if n % IMG_EVERY == 0:
            start(lambda side: halo_copy(n, side, 1))
            sent.append((n, 1))
        elif n > IMG_EVERY:
            wait_recv(lambda side: halo_copy(0, side, 1))
            save(0).start()
    for n in range(IMG_EVERY, STEPS + 1, IMG_EVERY):
        if n == STEPS:
            wait_recv(lambda side: halo_copy(n, side, 0))
        wait_recv(lambda side: halo_copy(n, side, 1))
        save(n).start()
    for which in range(3):
        wait_send(lambda side: model_copy(which, side))
    for n, chunk in sent:
        wait_send(lambda side: halo_copy(n, side, chunk))
    others(lambda j: t_send(j).wait_send())
    for n in range(0, STEPS + 1, IMG_EVERY):
        save(n).wait()


def imaging(levels_hbm, image_hbm, levels, image, in_sem, out_sem):
    rounds, rows = levels.shape[0], image.shape[1]
    loads = [pltpu.make_async_copy(levels_hbm.at[n], levels.at[n], in_sem.at[n]) for n in range(rounds)]
    for copy in loads:
        copy.start()
    for copy in loads:
        copy.wait()
    stores = []
    for start in range(0, NOFF, GROUP):
        for j in range(start, start + GROUP):
            shift = j - HALF

            def one(i, c, j=j, shift=shift):
                total = None
                for n in range(rounds):
                    product = levels[n, HALF + i - shift, 0] * levels[n, HALF + i + shift, 1]
                    total = product if total is None else total + product
                image[j, i] = total
                return c

            lax.fori_loop(0, rows, one, 0, unroll=True)
        part = pl.ds(start, GROUP)
        stores.append(pltpu.make_async_copy(image.at[part], image_hbm.at[part], out_sem.at[start // GROUP]))
        stores[-1].start()
    for copy in stores:
        copy.wait()


def solution(mesh):
    count = mesh.shape[AXIS]

    def local(sf, sp, rf, rp, stiff, buoy, wavelet, fire, shot, rcell, traces):
        rows, lateral, depth = sf.shape
        rounds = STEPS // IMG_EVERY
        wide = rows + 2 * HALF
        levels = pl.pallas_call(
            functools.partial(propagate, count),
            out_shape=jax.ShapeDtypeStruct((rounds + 1, wide, 2, lateral, depth), jnp.float32),
            in_specs=[pl.BlockSpec(memory_space=pltpu.HBM)] * 11,
            out_specs=pl.BlockSpec(memory_space=pltpu.HBM),
            scratch_shapes=[
                pltpu.VMEM((STEPS + 1, wide, 2, lateral, depth), jnp.float32),
                pltpu.VMEM((rows + 4 * REACH, lateral, depth), jnp.float32),
                pltpu.VMEM((25, rows + 2 * REACH, lateral, depth), jnp.float32),
                pltpu.VMEM(((rows + 2 * REACH) * lateral, 128), jnp.float32),
                pltpu.VMEM(((rows + 2 * REACH) * lateral, 128), jnp.float32),
                pltpu.VMEM((count,) + traces.shape, jnp.float32),
                pltpu.VMEM((wavelet.shape[1], 128), jnp.float32),
                pltpu.VMEM((8, 128), jnp.int32),
                pltpu.VMEM((rows + 2 * REACH, 2, lateral, depth), jnp.float32),
                pltpu.VMEM((rows + 2 * REACH, lateral, depth), jnp.float32),
                pltpu.VMEM(wavelet.shape[::-1], jnp.float32),
                pltpu.VMEM((1,) + fire.shape, jnp.int32),
                pltpu.VMEM((1,) + shot.shape, jnp.int32),
                pltpu.VMEM((count, traces.shape[1]), jnp.int32),
                pltpu.VMEM(traces.shape, jnp.float32),
                pltpu.SemaphoreType.DMA((11,)),
                pltpu.SemaphoreType.DMA((rounds + 1,)),
                pltpu.SemaphoreType.DMA((STEPS + 1, 2, 2)),
                pltpu.SemaphoreType.DMA((STEPS + 1, 2, 2)),
                pltpu.SemaphoreType.DMA((3, 2)),
                pltpu.SemaphoreType.DMA((3, 2)),
                pltpu.SemaphoreType.DMA((count,)),
                pltpu.SemaphoreType.DMA((count,)),
            ],
            compiler_params=pltpu.CompilerParams(
                collective_id=0, has_side_effects=True, vmem_limit_bytes=62 * 1024 * 1024),
        )(sf, sp, rf, rp, stiff, buoy, wavelet.T, fire.reshape(1, -1), shot.reshape(1, -1),
          rcell.reshape(count, traces.shape[1]), traces)
        hbm = pl.BlockSpec(memory_space=pltpu.HBM)
        return pl.pallas_call(
            imaging,
            out_shape=jax.ShapeDtypeStruct((NOFF, rows, lateral, depth), jnp.float32),
            in_specs=[hbm],
            out_specs=hbm,
            scratch_shapes=[
                pltpu.VMEM(levels.shape, jnp.float32),
                pltpu.VMEM((NOFF, rows, lateral, depth), jnp.float32),
                pltpu.SemaphoreType.DMA((rounds + 1,)),
                pltpu.SemaphoreType.DMA((NOFF // GROUP,)),
            ],
            compiler_params=pltpu.CompilerParams(vmem_limit_bytes=62 * 1024 * 1024),
        )(levels)

    placed = (
        P(("shot", AXIS), None, None),
        P(("shot", AXIS), None, None),
        P(("shot", AXIS), None, None),
        P(("shot", AXIS), None, None),
        P(AXIS, None, None),
        P(AXIS, None, None),
        P("shot", None),
        P("shot"),
        P("shot"),
        P("shot"),
        P("shot", AXIS),
    )
    return jax.shard_map(
        local, mesh=mesh, in_specs=placed, out_specs=P("shot", AXIS, None, None), check_vma=False
    )
```

```python
import functools
import math

import jax
import jax.numpy as jnp
from jax import lax
from jax.experimental import pallas as pl
from jax.experimental.pallas import tpu as pltpu
from jax.sharding import PartitionSpec as P

STEPS = 8
IMG_EVERY = 4
NOFF = 33
SURFACE = 4
HALF = 16
REACH = 4
AXIS = "gx"
UNROLL = 4
GROUP = 3

stencil_weights = (1.6, -0.2, 8.0 / 315.0, -1.0 / 560.0)


def split3(x):
    hi = x.astype(jnp.bfloat16)
    rest = x - hi.astype(jnp.float32)
    mid = rest.astype(jnp.bfloat16)
    low = (rest - mid.astype(jnp.float32)).astype(jnp.bfloat16)
    return hi, mid, low


def propagate(
    count,
    s_hbm, sp_hbm, r_hbm, rp_hbm, k_hbm, b_hbm, wave_hbm, fire_hbm, shot_hbm, rcell_hbm, trace_hbm,
    out_ref,
    lev, bx, coef, plane_s, plane_r, gathered, wpad, ipad,
    prior, k_ref, wave_ref, fire_ref, shot_ref, rcell_ref, trace_ref,
    in_sem, out_sem, send_sem, recv_sem, bsend_sem, brecv_sem, tsend_sem, trecv_sem,
):
    me = lax.axis_index(AXIS)
    rows, lateral, depth = s_hbm.shape
    H, E, D = HALF, REACH, 2 * REACH
    has_left, has_right = me > 0, me < count - 1

    def level(n):
        return lev.at[n]

    def save(n):
        return pltpu.make_async_copy(lev.at[n], out_ref.at[n // IMG_EVERY], out_sem.at[n // IMG_EVERY])

    first = level(0)
    loads = [
        pltpu.make_async_copy(src, dst, in_sem.at[i])
        for i, (src, dst) in enumerate((
            (trace_hbm, trace_ref),
            (b_hbm, bx.at[pl.ds(D, rows)]),
            (s_hbm, first.at[pl.ds(H, rows), 0]),
            (r_hbm, first.at[pl.ds(H, rows), 1]),
            (k_hbm, k_ref.at[pl.ds(E, rows)]),
            (wave_hbm, wave_ref),
            (fire_hbm, fire_ref),
            (shot_hbm, shot_ref),
            (rcell_hbm, rcell_ref),
            (sp_hbm, prior.at[pl.ds(E, rows), 0]),
            (rp_hbm, prior.at[pl.ds(E, rows), 1]),
        ))
    ]
    for copy in loads:
        copy.start()

    barrier = pltpu.get_barrier_semaphore()

    def greet(j, c):
        @pl.when(j != me)
        def _():
            pl.semaphore_signal(barrier, inc=1, device_id={AXIS: j}, device_id_type=pl.DeviceIdType.MESH)
        return c

    lax.fori_loop(0, count, greet, 0)

    zero_row = jnp.zeros((2, lateral, depth), jnp.float32)

    def blank(lo_halo):
        for n in range(0, STEPS + 1, 2):
            wide = H if n % IMG_EVERY == 0 else D
            at = H - wide if lo_halo else H + rows
            target = level(n)

            def one(i, c, target=target, at=at):
                target[at + i] = zero_row
                return c

            lax.fori_loop(0, wide, one, 0)

        def sides(i, c):
            at = i if lo_halo else E + rows + i
            prior[at] = zero_row
            k_ref[at] = zero_row[0]
            for part in range(2):
                bx[(part * E + i) if lo_halo else (D + rows + part * E + i)] = zero_row[0]
            return c

        lax.fori_loop(0, E, sides, 0)

    @pl.when(jnp.logical_not(has_left))
    def _():
        blank(True)

    @pl.when(jnp.logical_not(has_right))
    def _():
        blank(False)

    pl.semaphore_wait(barrier, count - 1)
    for copy in loads:
        copy.wait()
    gathered[me] = trace_ref[...]

    def shifted(ref, own, skip, size, side, send, recv):
        if side == 0:
            src, dst, to = own + rows - skip - size, own - skip - size, me + 1
        else:
            src, dst, to = own + skip, own + rows + skip, me - 1
        return pltpu.make_async_remote_copy(
            src_ref=ref.at[pl.ds(src, size)], dst_ref=ref.at[pl.ds(dst, size)],
            send_sem=send, recv_sem=recv,
            device_id={AXIS: to}, device_id_type=pl.DeviceIdType.MESH)

    def halo_copy(n, side, chunk):
        skip, size = (0, D) if chunk == 0 else (D, H - D)
        return shifted(level(n), H, skip, size, side, send_sem.at[n, side, chunk], recv_sem.at[n, side, chunk])

    def model_copy(which, side):
        ref, own, size = ((bx, D, D), (k_ref, E, E), (prior, E, E))[which]
        return shifted(ref, own, 0, size, side, bsend_sem.at[which, side], brecv_sem.at[which, side])

    def start(make, sides=(0, 1)):
        for side in sides:
            @pl.when((has_right, has_left)[side])
            def _(side=side):
                make(side).start()

    def wait_recv(make):
        @pl.when(has_left)
        def _():
            make(0).wait_recv()

        @pl.when(has_right)
        def _():
            make(1).wait_recv()

    def wait_send(make):
        @pl.when(has_right)
        def _():
            make(0).wait_send()

        @pl.when(has_left)
        def _():
            make(1).wait_send()

    def t_send(j):
        return pltpu.make_async_remote_copy(
            src_ref=trace_ref, dst_ref=gathered.at[me],
            send_sem=tsend_sem.at[j], recv_sem=trecv_sem.at[me],
            device_id={AXIS: j}, device_id_type=pl.DeviceIdType.MESH)

    def t_recv(j):
        return pltpu.make_async_remote_copy(
            src_ref=trace_ref, dst_ref=gathered.at[j],
            send_sem=tsend_sem.at[j], recv_sem=trecv_sem.at[j],
            device_id={AXIS: j}, device_id_type=pl.DeviceIdType.MESH)

    def others(act):
        def body(j, c):
            @pl.when(j != me)
            def _():
                act(j)
            return c

        lax.fori_loop(0, count, body, 0)

    others(lambda j: t_send(j).start())
    for which in range(2):
        start(lambda side: model_copy(which, side))
    start(lambda side: halo_copy(0, side, 0))
    start(lambda side: model_copy(2, side))

    lane = lax.broadcasted_iota(jnp.int32, (lateral, depth), 1)
    cross = lax.broadcasted_iota(jnp.int32, (lateral, depth), 0)

    def flat_coefs(i, c):
        b = bx[E + i]
        stiff = k_ref[i]
        total = jnp.zeros_like(b)
        for base, axis, index, length in ((8, 0, cross, lateral), (16, 1, lane, depth)):
            for k in range(1, REACH + 1):
                for s in (1, -1):
                    inside = index < length - k if s == 1 else index >= k
                    other = jnp.where(inside, pltpu.roll(b, (-s * k) % length, axis), 0.0)
                    t = (0.5 * stencil_weights[k - 1]) * (b + other)
                    total = total + t
                    coef[base + 2 * (k - 1) + (s < 0), i] = jnp.where(inside, stiff * t, 0.0)
        coef[24, i] = total
        return c

    lax.fori_loop(E, E + rows, flat_coefs, 0, unroll=2)

    def inline_coefs(i, c):
        b = bx[E + i]
        stiff = k_ref[i]
        total = coef[24, i]
        for k in range(1, REACH + 1):
            for s in (1, -1):
                t = (0.5 * stencil_weights[k - 1]) * (b + bx[E + i + s * k])
                total = total + t
                coef[2 * (k - 1) + (s < 0), i] = stiff * t
        coef[24, i] = 2.0 - stiff * total
        return c

    lax.fori_loop(D, rows, inline_coefs, 0, unroll=2)

    cells = (rows + D) * lateral
    cell_id = lax.broadcasted_iota(jnp.int32, (cells, 128), 0) + (me * rows - E) * lateral
    quiet = jnp.zeros((128 - 3 * STEPS, 128), jnp.bfloat16)

    def spread(cell_row, amounts):
        hot = jnp.where(cell_id == cell_row, 1.0, 0.0).astype(jnp.bfloat16)
        parts = jnp.concatenate(list(split3(amounts)) + [quiet], axis=0)
        return lax.dot_general(hot, parts, (((1,), (1,)), ((), ())), preferred_element_type=jnp.float32)

    def fold(p):
        return p + pltpu.roll(p, 128 - STEPS, 1) + pltpu.roll(p, 128 - 2 * STEPS, 1)

    samples, shots = wave_ref.shape
    wpad[...] = jnp.zeros_like(wpad)
    wpad[0:samples, 0:shots] = wave_ref[...]
    ipad[...] = jnp.full(ipad.shape, -1, jnp.int32)
    ipad[0:1, 0:shots] = fire_ref[...]
    ipad[1:2, 0:shots] = shot_ref[...]
    delay = lax.broadcasted_iota(jnp.int32, (STEPS, 128), 0) - ipad[0:1, :]
    amounts = jnp.zeros((STEPS, 128), jnp.float32)
    for d in range(samples):
        amounts = amounts + jnp.where(delay == d, wpad[d : d + 1, :], 0.0)
    plane_s[...] = fold(spread(ipad[1:2, :], amounts))

    others(lambda j: t_recv(j).wait_recv())
    plane_r[...] = jnp.zeros_like(plane_r)

    batch = math.gcd(count, 4)

    def absorb(q, c):
        total = None
        for part in range(batch):
            j = q * batch + part
            piece = spread(rcell_ref[pl.ds(j, 1), :], gathered[j])
            total = piece if total is None else total + piece
        plane_r[...] += total
        return c

    lax.fori_loop(0, count // batch, absorb, 0)
    plane_r[...] = fold(plane_r[...])

    wait_recv(lambda side: model_copy(0, side))
    wait_recv(lambda side: model_copy(1, side))

    def outer(q):
        return jnp.where(q < E, q, rows + q)

    def outer_coefs(q, c):
        flat_coefs(outer(q), c)
        inline_coefs(outer(q), c)
        return c

    def edge_coefs(q, c):
        return inline_coefs(jnp.where(q < E, q + E, rows - E + q), c)

    lax.fori_loop(0, D, outer_coefs, 0, unroll=2)
    lax.fori_loop(0, D, edge_coefs, 0, unroll=2)

    def advance(n, size, row):
        now, nxt = level(n), level(n + 1)

        def one(q, c):
            i = row(q)
            at = H - E + i
            for f in range(2):
                v = now[at, f]
                if n == 0:
                    before = prior[i, f]
                else:
                    before = level(n - 1)[at, f]
                acc = [coef[24, i] * v - before]
                for base, axis, length in ((8, 0, lateral), (16, 1, depth)):
                    part = None
                    for k in range(1, REACH + 1):
                        for s in (1, -1):
                            term = coef[base + 2 * (k - 1) + (s < 0), i] * pltpu.roll(v, (-s * k) % length, axis)
                            part = term if part is None else part + term
                    acc.append(part)
                part = None
                for k in range(1, REACH + 1):
                    for s in (1, -1):
                        term = coef[2 * (k - 1) + (s < 0), i] * now[at + s * k, f]
                        part = term if part is None else part + term
                acc.append(part)
                plane, column = (plane_s, n) if f == 0 else (plane_r, STEPS - 1 - n)
                p = plane[pl.ds(pl.multiple_of(i * lateral, lateral), lateral), :]
                p = jnp.where(lane == SURFACE, pltpu.roll(p, (SURFACE - column) % 128, 1), 0.0)
                nxt[at, f] = (acc[0] + acc[1]) + (acc[2] + acc[3]) + p
            return c

        lax.fori_loop(0, size, one, 0, unroll=UNROLL)

    sent = [(0, 0)]
    half = rows // 2
    for n in range(0, STEPS, 2):
        advance(n, rows - D, lambda q: D + q)
        wait_recv(lambda side: halo_copy(n, side, 0))
        if n == 0:
            wait_recv(lambda side: model_copy(2, side))
        advance(n, 2 * D, lambda q: jnp.where(q < D, q, rows - D + q))
        advance(n + 1, half, lambda q: E + q)
        start(lambda side: halo_copy(n + 2, side, 0), (1,))
        if n + 2 == STEPS:
            start(lambda side: halo_copy(n + 2, side, 1), (0,))
        advance(n + 1, rows - half, lambda q: E + half + q)
        start(lambda side: halo_copy(n + 2, side, 0), (0,))
        sent.append((n + 2, 0))
        if n + 2 == STEPS:
            start(lambda side: halo_copy(n + 2, side, 1), (1,))
            sent.append((n + 2, 1))
        if n % IMG_EVERY == 0:
            start(lambda side: halo_copy(n, side, 1))
            sent.append((n, 1))
        elif n > IMG_EVERY:
            wait_recv(lambda side: halo_copy(0, side, 1))
            save(0).start()
    for n in range(IMG_EVERY, STEPS + 1, IMG_EVERY):
        if n == STEPS:
            wait_recv(lambda side: halo_copy(n, side, 0))
        wait_recv(lambda side: halo_copy(n, side, 1))
        save(n).start()
    for which in range(3):
        wait_send(lambda side: model_copy(which, side))
    for n, chunk in sent:
        wait_send(lambda side: halo_copy(n, side, chunk))
    others(lambda j: t_send(j).wait_send())
    for n in range(0, STEPS + 1, IMG_EVERY):
        save(n).wait()


def imaging(levels_hbm, image_hbm, levels, image, in_sem, out_sem):
    rounds, rows = levels.shape[0], image.shape[1]
    loads = [pltpu.make_async_copy(levels_hbm.at[n], levels.at[n], in_sem.at[n]) for n in range(rounds)]
    for copy in loads:
        copy.start()
    for copy in loads:
        copy.wait()
    stores = []
    for start in range(0, NOFF, GROUP):
        for j in range(start, start + GROUP):
            shift = j - HALF

            def one(i, c, j=j, shift=shift):
                total = None
                for n in range(rounds):
                    product = levels[n, HALF + i - shift, 0] * levels[n, HALF + i + shift, 1]
                    total = product if total is None else total + product
                image[j, i] = total
                return c

            lax.fori_loop(0, rows, one, 0, unroll=True)
        part = pl.ds(start, GROUP)
        stores.append(pltpu.make_async_copy(image.at[part], image_hbm.at[part], out_sem.at[start // GROUP]))
        stores[-1].start()
    for copy in stores:
        copy.wait()


def solution(mesh):
    count = mesh.shape[AXIS]

    def local(sf, sp, rf, rp, stiff, buoy, wavelet, fire, shot, rcell, traces):
        rows, lateral, depth = sf.shape
        rounds = STEPS // IMG_EVERY
        wide = rows + 2 * HALF
        levels = pl.pallas_call(
            functools.partial(propagate, count),
            out_shape=jax.ShapeDtypeStruct((rounds + 1, wide, 2, lateral, depth), jnp.float32),
            in_specs=[pl.BlockSpec(memory_space=pltpu.HBM)] * 11,
            out_specs=pl.BlockSpec(memory_space=pltpu.HBM),
            scratch_shapes=[
                pltpu.VMEM((STEPS + 1, wide, 2, lateral, depth), jnp.float32),
                pltpu.VMEM((rows + 4 * REACH, lateral, depth), jnp.float32),
                pltpu.VMEM((25, rows + 2 * REACH, lateral, depth), jnp.float32),
                pltpu.VMEM(((rows + 2 * REACH) * lateral, 128), jnp.float32),
                pltpu.VMEM(((rows + 2 * REACH) * lateral, 128), jnp.float32),
                pltpu.VMEM((count,) + traces.shape, jnp.float32),
                pltpu.VMEM((wavelet.shape[1], 128), jnp.float32),
                pltpu.VMEM((8, 128), jnp.int32),
                pltpu.VMEM((rows + 2 * REACH, 2, lateral, depth), jnp.float32),
                pltpu.VMEM((rows + 2 * REACH, lateral, depth), jnp.float32),
                pltpu.VMEM(wavelet.shape[::-1], jnp.float32),
                pltpu.VMEM((1,) + fire.shape, jnp.int32),
                pltpu.VMEM((1,) + shot.shape, jnp.int32),
                pltpu.VMEM((count, traces.shape[1]), jnp.int32),
                pltpu.VMEM(traces.shape, jnp.float32),
                pltpu.SemaphoreType.DMA((11,)),
                pltpu.SemaphoreType.DMA((rounds + 1,)),
                pltpu.SemaphoreType.DMA((STEPS + 1, 2, 2)),
                pltpu.SemaphoreType.DMA((STEPS + 1, 2, 2)),
                pltpu.SemaphoreType.DMA((3, 2)),
                pltpu.SemaphoreType.DMA((3, 2)),
                pltpu.SemaphoreType.DMA((count,)),
                pltpu.SemaphoreType.DMA((count,)),
            ],
            compiler_params=pltpu.CompilerParams(
                collective_id=0, has_side_effects=True, vmem_limit_bytes=62 * 1024 * 1024),
        )(sf, sp, rf, rp, stiff, buoy, wavelet.T, fire.reshape(1, -1), shot.reshape(1, -1),
          rcell.reshape(count, traces.shape[1]), traces)
        hbm = pl.BlockSpec(memory_space=pltpu.HBM)
        return pl.pallas_call(
            imaging,
            out_shape=jax.ShapeDtypeStruct((NOFF, rows, lateral, depth), jnp.float32),
            in_specs=[hbm],
            out_specs=hbm,
            scratch_shapes=[
                pltpu.VMEM(levels.shape, jnp.float32),
                pltpu.VMEM((NOFF, rows, lateral, depth), jnp.float32),
                pltpu.SemaphoreType.DMA((rounds + 1,)),
                pltpu.SemaphoreType.DMA((NOFF // GROUP,)),
            ],
            compiler_params=pltpu.CompilerParams(vmem_limit_bytes=62 * 1024 * 1024),
        )(levels)

    placed = (
        P(("shot", AXIS), None, None),
        P(("shot", AXIS), None, None),
        P(("shot", AXIS), None, None),
        P(("shot", AXIS), None, None),
        P(AXIS, None, None),
        P(AXIS, None, None),
        P("shot", None),
        P("shot"),
        P("shot"),
        P("shot"),
        P("shot", AXIS),
    )
    return jax.shard_map(
        local, mesh=mesh, in_specs=placed, out_specs=P("shot", AXIS, None, None), check_vma=False
    )
```
